32 devices in a mesh: range: 16 (over z, y, core), height: 2 (over x).
Axes of the slice: x: 2, y: 2, z: 4, core: 2. Of those that a mesh axis runs over, the one named last changes fastest.
Arguments:
- acoustic: float32 [4, 128, 16, 512], P(None, 'range', 'height'), may hold values from -6 to 6
- mean_wind: float32 [3, 128, 16, 512], P(None, 'range', 'height'), may hold values from -0.72 to 0.72
- ground: int32 [128, 512], P('range'), may hold values from 0 to 4, as said below
- shifts: int32 [2], replicated, may hold values from 1 to 2, as said below
Outputs:
- evolved: float32 [4, 128, 16, 512], P(None, 'range', 'height')
The draws below stay inside these ranges and needn't reach their ends.
Inputs may be any that keep to these rules, and one draw needn't show every extreme that they name: `ground`: some column has exactly 4 solid cells. `shifts`: some step advances by exactly 2 rows.
All inputs are finite; a program needn't handle non-finite values.
Results may differ from the reference program's by a relative error of at most 0.00002.
Values sent between devices are 32-bit elements; how exact they have to be, the bound alone decides.
A program may use at most 64 MiB of HBM per device.

```python
import jax
import jax.numpy as jnp
from jax import lax

NY = 512
SMAX = 2
STEPS = 2
NX = 128
NZ = 16
GMAX = 4


def draw_ground(key, part):
    key_heights, key_row, key_column = jax.random.split(key, 3)
    heights = jax.random.randint(key_heights, (NX, NY), 0, GMAX + 1)
    row_pick = jax.random.randint(key_row, (), 0, NX)
    column_pick = jax.random.randint(key_column, (), 0, NY)
    return heights.at[row_pick, column_pick].set(GMAX).astype(jnp.int32)


def draw_shifts(key, part):
    key_values, key_pick = jax.random.split(key, 2)
    values = jax.random.randint(key_values, (STEPS,), 1, SMAX + 1)
    chosen = jax.random.randint(key_pick, (), 0, STEPS)
    return values.at[chosen].set(SMAX).astype(jnp.int32)


def shard_levels(stream_key, shape, pieces, low, top_value):
    loudness, own = 1.0, jax.random.fold_in(stream_key, 6)
    for dim, shards_of in pieces:
        steps = jnp.exp(jax.random.uniform(jax.random.fold_in(own, dim), (shards_of,), jnp.float32, low / len(pieces), top_value / len(pieces)))
        loudness = loudness * jnp.repeat(steps, shape[dim] // shards_of).reshape([-1 if axis == dim else 1 for axis in range(len(shape))])
    return loudness


def gaussian(stream_key, shape, deviation, limit, shards=(), kind=jnp.bfloat16):
    entries = deviation * jax.random.normal(stream_key, shape, jnp.float32)
    if shards:
        entries = entries * shard_levels(stream_key, shape, shards, -0.22, 0.18)
    return jnp.clip(entries, -limit, limit).astype(kind)


def setup_inputs(seed: int = 0) -> dict:
    key_list = jax.random.split(jax.random.key(seed), 5)
    acoustic = gaussian(key_list[0], (4, NX, NZ, NY), 1.0, 6.0, ((1, 16), (2, 2)), jnp.float32)
    mean_wind = gaussian(key_list[1], (3, NX, NZ, NY), 0.12, 0.72, ((1, 16), (2, 2)), jnp.float32)
    ground = draw_ground(jax.random.fold_in(key_list[4], 71), 0)
    shifts = draw_shifts(jax.random.fold_in(key_list[4], 71), 0)
    return dict(acoustic=acoustic, mean_wind=mean_wind, ground=ground, shifts=shifts)


FRAME_SPEED = 1.0
TIME_STEP = 0.4
HALF_STEP = 0.2
SIXTH_STEP = 0.4 / 6.0


def central(blocked, along, extent):
    def window(offset):
        return lax.slice_in_dim(blocked, offset, offset + extent, axis=along)
    return (8.0 * (window(3) - window(1)) - (window(4) - window(0))) / 12.0


def tendency(padded, wind_now):
    range_rows = wind_now.shape[1]
    levels = wind_now.shape[2]
    centre = padded[:, 2:range_rows + 2, 2:levels + 2, :]
    slope_range = central(padded[:, :, 2:levels + 2, :], 1, range_rows)
    slope_height = central(padded[:, 2:range_rows + 2, :, :], 2, levels)
    slope_cross = central(jnp.pad(centre, ((0, 0), (0, 0), (0, 0), (2, 2))), 3, centre.shape[3])
    carried = (wind_now[0] - FRAME_SPEED) * slope_range + wind_now[1] * slope_cross + wind_now[2] * slope_height
    pressure = -carried[0] - (slope_range[1] + slope_cross[2] + slope_height[3])
    along_range = -carried[1] - slope_range[0]
    along_cross = -carried[2] - slope_cross[0]
    upward = -carried[3] - slope_height[0]
    return jnp.stack([pressure, along_range, along_cross, upward])


def advance(state, wind_now, keep_mask):
    def slope(field):
        return tendency(jnp.pad(field, ((0, 0), (2, 2), (2, 2), (0, 0))), wind_now)
    first_slope = slope(state)
    second_state = (state + HALF_STEP * first_slope) * keep_mask
    second_slope = slope(second_state)
    third_state = (state + HALF_STEP * second_slope) * keep_mask
    third_slope = slope(third_state)
    fourth_state = (state + TIME_STEP * third_slope) * keep_mask
    fourth_slope = slope(fourth_state)
    total = first_slope + 2.0 * second_slope + 2.0 * third_slope + fourth_slope
    return (state + SIXTH_STEP * total) * keep_mask


def reference(acoustic, mean_wind, ground, shifts):
    heights = jnp.arange(NZ, dtype=jnp.int32)
    fluid = (heights[None, :, None] >= ground[:, None, :]).astype(jnp.float32)
    medium = jnp.concatenate([mean_wind, fluid[None]], axis=0)
    state = acoustic
    for step_index in range(STEPS):
        widened = jnp.concatenate([medium, medium[:, :SMAX]], axis=1)
        medium = lax.dynamic_slice_in_dim(widened, shifts[step_index].astype(jnp.int32), NX, 1)
        state = advance(state, medium[:3], medium[3])
    return state
```

```python
import functools

import jax
import jax.numpy as jnp
from jax import lax
from jax.experimental import pallas as pl
from jax.experimental.pallas import tpu as pltpu
from jax.sharding import PartitionSpec as P

SMAX = 2
MESH = pl.DeviceIdType.MESH
LANES = 128
SUB = 8


def kernel(
    n_range, n_height, steps,
    shifts_ref, a_ref, w_in, g_in, o_ref,
    cur, base, acc, wind, mask, ground, pack, halo, send_sem, recv_sem, wsend, wrecv,
):
    rows, levels, width = a_ref.shape[1], a_ref.shape[2], a_ref.shape[3]
    tiles, blocks = levels // SUB, width // LANES
    extra = SMAX * steps
    me, hi = lax.axis_index("range"), lax.axis_index("height")
    below, above = me - 1, me + 1
    wrap_below = lax.rem(me + n_range - 1, n_range)
    wrap_above = lax.rem(me + 1, n_range)
    has_below, has_above = me > 0, me < n_range - 1
    has_down, has_up = hi > 0, hi < n_height - 1

    sub = lax.broadcasted_iota(jnp.int32, (SUB, LANES), 0)
    lane = lax.broadcasted_iota(jnp.int32, (SUB, LANES), 1)

    barrier = pltpu.get_barrier_semaphore()
    pl.semaphore_signal(barrier, inc=1, device_id={"range": wrap_below}, device_id_type=MESH)
    pl.semaphore_signal(barrier, inc=1, device_id={"range": wrap_above}, device_id_type=MESH)

    @pl.when(has_down)
    def _():
        pl.semaphore_signal(barrier, inc=1, device_id={"height": hi - 1}, device_id_type=MESH)

    @pl.when(has_up)
    def _():
        pl.semaphore_signal(barrier, inc=1, device_id={"height": hi + 1}, device_id_type=MESH)

    def pack_row(slot, field, row, low, high):
        down, up = low[0], None
        for j in range(blocks):
            up_j = pltpu.roll(high[j], (2 * j - (SUB - 2)) % SUB, 0)
            if j == 0:
                up = up_j
                continue
            here = (sub >= 2 * j)
            down = jnp.where(here, pltpu.roll(low[j], 2 * j, 0), down)
            up = jnp.where(here, up_j, up)
        pack[slot, 0, field, row] = down
        pack[slot, 1, field, row] = up

    def load_row(row, carry):
        for f in range(4):
            for t in range(tiles):
                cur[0, f, row + 2, t * SUB:(t + 1) * SUB, :] = a_ref[f, row, t * SUB:(t + 1) * SUB, :]
            low = [a_ref[f, row, 0:SUB, j * LANES:(j + 1) * LANES] for j in range(blocks)]
            high = [a_ref[f, row, levels - SUB:levels, j * LANES:(j + 1) * LANES] for j in range(blocks)]
            pack_row(0, f, row, low, high)
        return carry

    lax.fori_loop(0, rows, load_row, 0)

    nothing = jnp.zeros((SUB, width), jnp.float32)

    @pl.when(jnp.logical_not(has_below))
    def _():
        for s in range(2):
            for f in range(4):
                for r in range(2):
                    for t in range(tiles):
                        cur[s, f, r, t * SUB:(t + 1) * SUB, :] = nothing

    @pl.when(jnp.logical_not(has_above))
    def _():
        for s in range(2):
            for f in range(4):
                for r in range(2):
                    for t in range(tiles):
                        cur[s, f, rows + 2 + r, t * SUB:(t + 1) * SUB, :] = nothing

    small = jnp.zeros((SUB, LANES), jnp.float32)

    @pl.when(jnp.logical_not(has_down))
    def _():
        for s in range(2):
            for f in range(4):
                for r in range(rows):
                    halo[s, 0, f, r] = small

    @pl.when(jnp.logical_not(has_up))
    def _():
        for s in range(2):
            for f in range(4):
                for r in range(rows):
                    halo[s, 1, f, r] = small

    pl.semaphore_wait(barrier, 2 + has_down.astype(jnp.int32) + has_up.astype(jnp.int32))

    def to_below(slot):
        return pltpu.make_async_remote_copy(
            src_ref=cur.at[slot, :, pl.ds(2, 2)], dst_ref=cur.at[slot, :, pl.ds(rows + 2, 2)],
            send_sem=send_sem.at[slot, 0], recv_sem=recv_sem.at[slot, 0],
            device_id={"range": below}, device_id_type=MESH)

    def to_above(slot):
        return pltpu.make_async_remote_copy(
            src_ref=cur.at[slot, :, pl.ds(rows, 2)], dst_ref=cur.at[slot, :, pl.ds(0, 2)],
            send_sem=send_sem.at[slot, 1], recv_sem=recv_sem.at[slot, 1],
            device_id={"range": above}, device_id_type=MESH)

    spans = [(0, 2), (2, rows - 4), (rows - 2, 2)]

    def to_down(slot, part):
        first, count = spans[part]
        return pltpu.make_async_remote_copy(
            src_ref=pack.at[slot, 0, :, pl.ds(first, count)], dst_ref=halo.at[slot, 1, :, pl.ds(first, count)],
            send_sem=send_sem.at[slot, 2 + part], recv_sem=recv_sem.at[slot, 2 + part],
            device_id={"height": hi - 1}, device_id_type=MESH)

    def to_up(slot, part):
        first, count = spans[part]
        return pltpu.make_async_remote_copy(
            src_ref=pack.at[slot, 1, :, pl.ds(first, count)], dst_ref=halo.at[slot, 0, :, pl.ds(first, count)],
            send_sem=send_sem.at[slot, 5 + part], recv_sem=recv_sem.at[slot, 5 + part],
            device_id={"height": hi + 1}, device_id_type=MESH)

    def send_height(slot, part):
        pl.when(has_down)(lambda: to_down(slot, part).start())
        pl.when(has_up)(lambda: to_up(slot, part).start())

    def recv_height(slot, part):
        pl.when(has_up)(lambda: to_down(slot, part).wait_recv())
        pl.when(has_down)(lambda: to_up(slot, part).wait_recv())

    def drain(slot):
        def down():
            for part in range(3):
                to_down(slot, part).wait_send()

        def up():
            for part in range(3):
                to_up(slot, part).wait_send()

        pl.when(has_below)(lambda: to_below(slot).wait_send())
        pl.when(has_above)(lambda: to_above(slot).wait_send())
        pl.when(has_down)(down)
        pl.when(has_up)(up)

    def wind_copy(step):
        return pltpu.make_async_remote_copy(
            src_ref=w_in.at[:, pl.ds(SMAX * step, SMAX)], dst_ref=wind.at[:, pl.ds(rows + SMAX * step, SMAX)],
            send_sem=wsend.at[step], recv_sem=wrecv.at[step],
            device_id={"range": wrap_below}, device_id_type=MESH)

    ground_copy = pltpu.make_async_remote_copy(
        src_ref=g_in, dst_ref=ground, send_sem=wsend.at[steps], recv_sem=wrecv.at[steps],
        device_id={"range": wrap_below}, device_id_type=MESH)

    pl.when(has_below)(lambda: to_below(0).start())
    pl.when(has_above)(lambda: to_above(0).start())
    for part in (1, 0, 2):
        send_height(0, part)
    ground_copy.start()
    for step in range(steps):
        wind_copy(step).start()

    def own_wind(row, carry):
        for c in range(3):
            for t in range(tiles):
                wind[c, row, t * SUB:(t + 1) * SUB, :] = w_in[c, row, t * SUB:(t + 1) * SUB, :]
        return carry

    lax.fori_loop(0, rows, own_wind, 0)
    level = lax.broadcasted_iota(jnp.int32, (SUB, width), 0) + hi * levels

    def flags(row, solid):
        for t in range(tiles):
            mask[row, t * SUB:(t + 1) * SUB, :] = jnp.where(level + t * SUB >= solid, 1.0, 0.0)

    for r in range(rows):
        flags(r, g_in[r:r + 1, :])
    ground_copy.wait_recv()
    for r in range(extra):
        flags(rows + r, ground[r:r + 1, :])

    def stage_row(row, k, step, slot, offset):
        nxt = 1 - slot
        stage = k % 4
        made = {}
        for t in range(tiles):
            level_at = slice(t * SUB, (t + 1) * SUB)
            for j in range(blocks):
                at = slice(j * LANES, (j + 1) * LANES)
                slopes = []
                for f in range(4):
                    c = cur[slot, f, row + 2, level_at, at]
                    d_r = 8.0 * (cur[slot, f, row + 3, level_at, at] - cur[slot, f, row + 1, level_at, at]) - (
                        cur[slot, f, row + 4, level_at, at] - cur[slot, f, row, level_at, at])
                    if j + 1 < blocks:
                        right = cur[slot, f, row + 2, level_at, (j + 1) * LANES:(j + 2) * LANES]
                    else:
                        right = small
                    if j:
                        left = cur[slot, f, row + 2, level_at, (j - 1) * LANES:j * LANES]
                    else:
                        left = small
                    p1 = pltpu.roll(jnp.where(lane < 1, right, c), LANES - 1, 1)
                    p2 = pltpu.roll(jnp.where(lane < 2, right, c), LANES - 2, 1)
                    m1 = pltpu.roll(jnp.where(lane >= LANES - 1, left, c), 1, 1)
                    m2 = pltpu.roll(jnp.where(lane >= LANES - 2, left, c), 2, 1)
                    d_c = 8.0 * (p1 - m1) - (p2 - m2)
                    if t + 1 < tiles:
                        top = cur[slot, f, row + 2, (t + 1) * SUB:(t + 2) * SUB, at]
                    else:
                        top = halo[slot, 1, f, row]
                        if j:
                            top = pltpu.roll(top, SUB - 2 * j, 0)
                    if t:
                        foot = cur[slot, f, row + 2, (t - 1) * SUB:t * SUB, at]
                    else:
                        foot = halo[slot, 0, f, row]
                        if (SUB - 2 - 2 * j) % SUB:
                            foot = pltpu.roll(foot, (SUB - 2 - 2 * j) % SUB, 0)
                    p1 = pltpu.roll(jnp.where(sub < 1, top, c), SUB - 1, 0)
                    p2 = pltpu.roll(jnp.where(sub < 2, top, c), SUB - 2, 0)
                    m1 = pltpu.roll(jnp.where(sub >= SUB - 1, foot, c), 1, 0)
                    m2 = pltpu.roll(jnp.where(sub >= SUB - 2, foot, c), 2, 0)
                    d_h = 8.0 * (p1 - m1) - (p2 - m2)
                    slopes.append((d_r, d_c, d_h))
                a_r = wind[0, row + offset, level_at, at] - 1.0
                a_c = wind[1, row + offset, level_at, at]
                a_h = wind[2, row + offset, level_at, at]
                fluid = mask[row + offset, level_at, at]
                p, u, v, w = slopes
                direct = [u[0] + v[1] + w[2], p[0], p[1], p[2]]
                for f in range(4):
                    d_r, d_c, d_h = slopes[f]
                    change = a_r * d_r + a_c * d_c + a_h * d_h + direct[f]
                    start = (a_ref if step == 0 else base)[f, row, level_at, at]
                    if stage == 0:
                        acc[f, row, level_at, at] = change
                    elif stage < 3:
                        acc[f, row, level_at, at] = acc[f, row, level_at, at] + 2.0 * change
                    if stage < 3:
                        new = (start - ((0.4 if stage == 2 else 0.2) / 12.0) * change) * fluid
                    else:
                        new = (start - (0.4 / 72.0) * (acc[f, row, level_at, at] + change)) * fluid
                    if k == 4 * steps - 1:
                        o_ref[f, row, level_at, at] = new
                        continue
                    if stage == 3:
                        base[f, row, level_at, at] = new
                    cur[nxt, f, row + 2, level_at, at] = new
                    made[f, t, j] = new
        if k < 4 * steps - 1:
            for f in range(4):
                pack_row(
                    nxt, f, row,
                    [made[f, 0, j] for j in range(blocks)], [made[f, tiles - 1, j] for j in range(blocks)])

    last = 4 * steps - 1
    offset = 0
    for k in range(4 * steps):
        step, slot = k // 4, k % 2
        nxt = 1 - slot
        if k % 4 == 0:
            offset = offset + shifts_ref[step]
        if k == 0:
            for later in range(steps):
                wind_copy(later).wait_recv()
        if k >= 1:
            drain(nxt)
        offset_now = offset

        def run(part, k=k, step=step, slot=slot, offset_now=offset_now):
            first, count = spans[part]

            def body(i, carry):
                stage_row(first + i, k, step, slot, offset_now)
                return carry

            lax.fori_loop(0, count, body, 0)

        recv_height(slot, 1)
        run(1)
        if k < last:
            send_height(nxt, 1)
        recv_height(slot, 0)
        pl.when(has_below)(lambda slot=slot: to_above(slot).wait_recv())
        run(0)
        if k < last:
            pl.when(has_below)(lambda nxt=nxt: to_below(nxt).start())
            send_height(nxt, 0)
        recv_height(slot, 2)
        pl.when(has_above)(lambda slot=slot: to_below(slot).wait_recv())
        run(2)
        if k < last:
            pl.when(has_above)(lambda nxt=nxt: to_above(nxt).start())
            send_height(nxt, 2)
    drain(last % 2)
    for step in range(steps):
        wind_copy(step).wait_send()
    ground_copy.wait_send()


def on_device(n_range, n_height, acoustic, mean_wind, ground, shifts):
    _, rows, levels, width = acoustic.shape
    steps = shifts.shape[0]
    vmem = pl.BlockSpec(memory_space=pltpu.VMEM)
    return pl.pallas_call(
        functools.partial(kernel, n_range, n_height, steps),
        out_shape=jax.ShapeDtypeStruct(acoustic.shape, jnp.float32),
        in_specs=[pl.BlockSpec(memory_space=pltpu.SMEM), vmem, vmem, vmem],
        out_specs=vmem,
        scratch_shapes=[
            pltpu.VMEM((2, 4, rows + 4, levels, width), jnp.float32),
            pltpu.VMEM(acoustic.shape, jnp.float32),
            pltpu.VMEM(acoustic.shape, jnp.float32),
            pltpu.VMEM((3, rows + SMAX * steps, levels, width), jnp.float32),
            pltpu.VMEM((rows + SMAX * steps, levels, width), jnp.float32),
            pltpu.VMEM((rows, width), jnp.int32),
            pltpu.VMEM((2, 2, 4, rows, SUB, LANES), jnp.float32),
            pltpu.VMEM((2, 2, 4, rows, SUB, LANES), jnp.float32),
            pltpu.SemaphoreType.DMA((2, 8)),
            pltpu.SemaphoreType.DMA((2, 8)),
            pltpu.SemaphoreType.DMA((steps + 1,)),
            pltpu.SemaphoreType.DMA((steps + 1,)),
        ],
        compiler_params=pltpu.CompilerParams(
            collective_id=0, has_side_effects=True, vmem_limit_bytes=40 * 1024 * 1024),
    )(shifts, acoustic, mean_wind, ground)


def solution(mesh):
    spec = P(None, "range", "height", None)
    return jax.shard_map(
        functools.partial(on_device, mesh.shape["range"], mesh.shape["height"]),
        mesh=mesh, in_specs=(spec, spec, P("range", None), P()), out_specs=spec, check_vma=False)
```

```python
import functools

import jax
import jax.numpy as jnp
from jax import lax
from jax.experimental import pallas as pl
from jax.experimental.pallas import tpu as pltpu
from jax.sharding import PartitionSpec as P

SMAX = 2
MESH = pl.DeviceIdType.MESH
LANES = 128
SUB = 8


def kernel(
    n_range, n_height, steps,
    shifts_ref, a_ref, w_in, g_in, o_ref,
    cur, base, acc, own, top, wind, mask, solid, ground, pack, halo, send_sem, recv_sem, wsend, wrecv, local,
):
    rows, levels, width = a_ref.shape[1], a_ref.shape[2], a_ref.shape[3]
    tiles, blocks = levels // SUB, width // LANES
    extra = SMAX * steps
    me, hi = lax.axis_index("range"), lax.axis_index("height")
    below, above = me - 1, me + 1
    wrap_below = lax.rem(me + n_range - 1, n_range)
    wrap_above = lax.rem(me + 1, n_range)
    has_below, has_above = me > 0, me < n_range - 1
    has_down, has_up = hi > 0, hi < n_height - 1

    sub = lax.broadcasted_iota(jnp.int32, (SUB, LANES), 0)
    lane = lax.broadcasted_iota(jnp.int32, (SUB, LANES), 1)

    fetches = [
        pltpu.make_async_copy(a_ref, cur.at[0, :, pl.ds(2, rows)], local.at[0]),
        pltpu.make_async_copy(g_in, solid, local.at[1]),
        pltpu.make_async_copy(a_ref, base, local.at[2]),
        pltpu.make_async_copy(w_in, own, local.at[3]),
        pltpu.make_async_copy(w_in.at[:, pl.ds(rows - 2, 2)], top.at[:, pl.ds(0, 2)], local.at[4]),
        pltpu.make_async_copy(w_in, wind.at[:, pl.ds(0, rows)], local.at[5]),
    ]
    barrier = pltpu.get_barrier_semaphore()
    pl.semaphore_signal(barrier, inc=1, device_id={"range": wrap_below}, device_id_type=MESH)
    pl.semaphore_signal(barrier, inc=1, device_id={"range": wrap_above}, device_id_type=MESH)

    @pl.when(has_down)
    def _():
        pl.semaphore_signal(barrier, inc=1, device_id={"height": hi - 1}, device_id_type=MESH)

    @pl.when(has_up)
    def _():
        pl.semaphore_signal(barrier, inc=1, device_id={"height": hi + 1}, device_id_type=MESH)

    for fetch in fetches:
        fetch.start()

    def pack_row(slot, field, row, low, high):
        down, up = low[0], None
        for j in range(blocks):
            up_j = pltpu.roll(high[j], (2 * j - (SUB - 2)) % SUB, 0)
            if j == 0:
                up = up_j
                continue
            here = (sub >= 2 * j)
            down = jnp.where(here, pltpu.roll(low[j], 2 * j, 0), down)
            up = jnp.where(here, up_j, up)
        pack[slot, 0, field, row] = down
        pack[slot, 1, field, row] = up

    nothing = jnp.zeros((SUB, width), jnp.float32)

    @pl.when(jnp.logical_not(has_below))
    def _():
        for s in range(2):
            for f in range(4):
                for r in range(2):
                    for t in range(tiles):
                        cur[s, f, r, t * SUB:(t + 1) * SUB, :] = nothing

    @pl.when(jnp.logical_not(has_above))
    def _():
        for s in range(2):
            for f in range(4):
                for r in range(2):
                    for t in range(tiles):
                        cur[s, f, rows + 2 + r, t * SUB:(t + 1) * SUB, :] = nothing

    small = jnp.zeros((SUB, LANES), jnp.float32)

    @pl.when(jnp.logical_not(has_down))
    def _():
        for s in range(2):
            for f in range(4):
                for r in range(rows):
                    halo[s, 0, f, r] = small

    @pl.when(jnp.logical_not(has_up))
    def _():
        for s in range(2):
            for f in range(4):
                for r in range(rows):
                    halo[s, 1, f, r] = small

    level = lax.broadcasted_iota(jnp.int32, (SUB, width), 0) + hi * levels

    def flags(row, foot):
        for t in range(tiles):
            mask[row, t * SUB:(t + 1) * SUB, :] = jnp.where(level + t * SUB >= foot, 1.0, 0.0)

    def load_row(row, carry):
        for f in range(4):
            low = [cur[0, f, row + 2, 0:SUB, j * LANES:(j + 1) * LANES] for j in range(blocks)]
            high = [cur[0, f, row + 2, levels - SUB:levels, j * LANES:(j + 1) * LANES] for j in range(blocks)]
            pack_row(0, f, row, low, high)
        return carry

    fetches[0].wait()
    lax.fori_loop(0, rows, load_row, 0)
    fetches[1].wait()
    for r in range(rows):
        flags(r, solid[r:r + 1, :])
    pl.semaphore_wait(barrier, 2 + has_down.astype(jnp.int32) + has_up.astype(jnp.int32))

    def to_below(slot):
        return pltpu.make_async_remote_copy(
            src_ref=cur.at[slot, :, pl.ds(2, 2)], dst_ref=cur.at[slot, :, pl.ds(rows + 2, 2)],
            send_sem=send_sem.at[slot, 0], recv_sem=recv_sem.at[slot, 0],
            device_id={"range": below}, device_id_type=MESH)

    def to_above(slot):
        return pltpu.make_async_remote_copy(
            src_ref=cur.at[slot, :, pl.ds(rows, 2)], dst_ref=cur.at[slot, :, pl.ds(0, 2)],
            send_sem=send_sem.at[slot, 1], recv_sem=recv_sem.at[slot, 1],
            device_id={"range": above}, device_id_type=MESH)

    spans = [(0, 2), (2, rows - 4), (rows - 2, 2)]

    def to_down(slot, part):
        first, count = spans[part]
        return pltpu.make_async_remote_copy(
            src_ref=pack.at[slot, 0, :, pl.ds(first, count)], dst_ref=halo.at[slot, 1, :, pl.ds(first, count)],
            send_sem=send_sem.at[slot, 2 + part], recv_sem=recv_sem.at[slot, 2 + part],
            device_id={"height": hi - 1}, device_id_type=MESH)

    def to_up(slot, part):
        first, count = spans[part]
        return pltpu.make_async_remote_copy(
            src_ref=pack.at[slot, 1, :, pl.ds(first, count)], dst_ref=halo.at[slot, 0, :, pl.ds(first, count)],
            send_sem=send_sem.at[slot, 5 + part], recv_sem=recv_sem.at[slot, 5 + part],
            device_id={"height": hi + 1}, device_id_type=MESH)

    def send_height(slot, part):
        pl.when(has_down)(lambda: to_down(slot, part).start())
        pl.when(has_up)(lambda: to_up(slot, part).start())

    def recv_height(slot, part):
        pl.when(has_up)(lambda: to_down(slot, part).wait_recv())
        pl.when(has_down)(lambda: to_up(slot, part).wait_recv())

    def drain(slot):
        def down():
            for part in range(3):
                to_down(slot, part).wait_send()

        def up():
            for part in range(3):
                to_up(slot, part).wait_send()

        pl.when(has_below)(lambda: to_below(slot).wait_send())
        pl.when(has_above)(lambda: to_above(slot).wait_send())
        pl.when(has_down)(down)
        pl.when(has_up)(up)

    wind_first = pltpu.make_async_remote_copy(
        src_ref=w_in.at[:, pl.ds(0, SMAX)], dst_ref=top.at[:, pl.ds(2, SMAX)],
        send_sem=wsend.at[0], recv_sem=wrecv.at[0],
        device_id={"range": wrap_below}, device_id_type=MESH)
    wind_rest = pltpu.make_async_remote_copy(
        src_ref=w_in.at[:, pl.ds(SMAX, extra - SMAX)], dst_ref=wind.at[:, pl.ds(rows + SMAX, extra - SMAX)],
        send_sem=wsend.at[1], recv_sem=wrecv.at[1],
        device_id={"range": wrap_below}, device_id_type=MESH)
    ground_copy = pltpu.make_async_remote_copy(
        src_ref=g_in, dst_ref=ground, send_sem=wsend.at[2], recv_sem=wrecv.at[2],
        device_id={"range": wrap_below}, device_id_type=MESH)

    pl.when(has_below)(lambda: to_below(0).start())
    pl.when(has_above)(lambda: to_above(0).start())
    for part in (1, 0, 2):
        send_height(0, part)
    ground_copy.start()
    wind_first.start()
    fetches[2].wait()
    fetches[3].wait()

    def stage_row(row, k, step, slot, offset, air, air_row):
        nxt = 1 - slot
        stage = k % 4
        made = {}
        for t in range(tiles):
            level_at = slice(t * SUB, (t + 1) * SUB)
            for j in range(blocks):
                at = slice(j * LANES, (j + 1) * LANES)
                slopes = []
                for f in range(4):
                    c = cur[slot, f, row + 2, level_at, at]
                    d_r = 8.0 * (cur[slot, f, row + 3, level_at, at] - cur[slot, f, row + 1, level_at, at]) - (
                        cur[slot, f, row + 4, level_at, at] - cur[slot, f, row, level_at, at])
                    if j + 1 < blocks:
                        right = cur[slot, f, row + 2, level_at, (j + 1) * LANES:(j + 2) * LANES]
                    else:
                        right = small
                    if j:
                        left = cur[slot, f, row + 2, level_at, (j - 1) * LANES:j * LANES]
                    else:
                        left = small
                    p1 = pltpu.roll(jnp.where(lane < 1, right, c), LANES - 1, 1)
                    p2 = pltpu.roll(jnp.where(lane < 2, right, c), LANES - 2, 1)
                    m1 = pltpu.roll(jnp.where(lane >= LANES - 1, left, c), 1, 1)
                    m2 = pltpu.roll(jnp.where(lane >= LANES - 2, left, c), 2, 1)
                    d_c = 8.0 * (p1 - m1) - (p2 - m2)
                    if t + 1 < tiles:
                        top = cur[slot, f, row + 2, (t + 1) * SUB:(t + 2) * SUB, at]
                    else:
                        top = halo[slot, 1, f, row]
                        if j:
                            top = pltpu.roll(top, SUB - 2 * j, 0)
                    if t:
                        foot = cur[slot, f, row + 2, (t - 1) * SUB:t * SUB, at]
                    else:
                        foot = halo[slot, 0, f, row]
                        if (SUB - 2 - 2 * j) % SUB:
                            foot = pltpu.roll(foot, (SUB - 2 - 2 * j) % SUB, 0)
                    p1 = pltpu.roll(jnp.where(sub < 1, top, c), SUB - 1, 0)
                    p2 = pltpu.roll(jnp.where(sub < 2, top, c), SUB - 2, 0)
                    m1 = pltpu.roll(jnp.where(sub >= SUB - 1, foot, c), 1, 0)
                    m2 = pltpu.roll(jnp.where(sub >= SUB - 2, foot, c), 2, 0)
                    d_h = 8.0 * (p1 - m1) - (p2 - m2)
                    slopes.append((d_r, d_c, d_h))
                a_r = air[0, air_row, level_at, at] - 1.0
                a_c = air[1, air_row, level_at, at]
                a_h = air[2, air_row, level_at, at]
                fluid = mask[row + offset, level_at, at]
                p, u, v, w = slopes
                direct = [u[0] + v[1] + w[2], p[0], p[1], p[2]]
                for f in range(4):
                    d_r, d_c, d_h = slopes[f]
                    change = a_r * d_r + a_c * d_c + a_h * d_h + direct[f]
                    start = base[f, row, level_at, at]
                    if stage == 0:
                        acc[f, row, level_at, at] = change
                    elif stage < 3:
                        acc[f, row, level_at, at] = acc[f, row, level_at, at] + 2.0 * change
                    if stage < 3:
                        new = (start - ((0.4 if stage == 2 else 0.2) / 12.0) * change) * fluid
                    else:
                        new = (start - (0.4 / 72.0) * (acc[f, row, level_at, at] + change)) * fluid
                    if stage == 3 and k < 4 * steps - 1:
                        base[f, row, level_at, at] = new
                    cur[nxt, f, row + 2, level_at, at] = new
                    made[f, t, j] = new
        if k < 4 * steps - 1:
            for f in range(4):
                pack_row(
                    nxt, f, row,
                    [made[f, 0, j] for j in range(blocks)], [made[f, tiles - 1, j] for j in range(blocks)])

    last = 4 * steps - 1
    results = [
        pltpu.make_async_copy(
            cur.at[1 - last % 2, :, pl.ds(2 + first, count)], o_ref.at[:, pl.ds(first, count)], local.at[6 + part])
        for part, (first, count) in enumerate(spans)
    ]
    offset = 0
    for k in range(4 * steps):
        step, slot = k // 4, k % 2
        nxt = 1 - slot
        if k % 4 == 0:
            offset = offset + shifts_ref[step]
        if k == 4:
            fetches[5].wait()
            wind_rest.wait_recv()
            for c in range(3):
                for r in range(SMAX):
                    for t in range(tiles):
                        wind[c, rows + r, t * SUB:(t + 1) * SUB, :] = top[c, 2 + r, t * SUB:(t + 1) * SUB, :]
        if k >= 1:
            drain(nxt)
        offset_now = offset

        def run(part, k=k, step=step, slot=slot, offset_now=offset_now):
            first, count = spans[part]

            def body(i, carry):
                row = first + i
                if step:
                    stage_row(row, k, step, slot, offset_now, wind, row + offset_now)
                elif part < 2:
                    stage_row(row, k, step, slot, offset_now, own, row + offset_now)
                else:
                    stage_row(row, k, step, slot, offset_now, top, row + offset_now - (rows - 2))
                return carry

            lax.fori_loop(0, count, body, 0)

        recv_height(slot, 1)
        run(1)
        if k < last:
            send_height(nxt, 1)
        else:
            results[1].start()
        if k == 1:
            wind_rest.start()
        recv_height(slot, 0)
        pl.when(has_below)(lambda slot=slot: to_above(slot).wait_recv())
        run(0)
        if k < last:
            pl.when(has_below)(lambda nxt=nxt: to_below(nxt).start())
            send_height(nxt, 0)
        else:
            results[0].start()
        recv_height(slot, 2)
        pl.when(has_above)(lambda slot=slot: to_below(slot).wait_recv())
        if k == 0:
            fetches[4].wait()
            wind_first.wait_recv()
            ground_copy.wait_recv()
            for r in range(extra):
                flags(rows + r, ground[r:r + 1, :])
        run(2)
        if k < last:
            pl.when(has_above)(lambda nxt=nxt: to_above(nxt).start())
            send_height(nxt, 2)
        else:
            results[2].start()
    drain(last % 2)
    for copy in (wind_first, wind_rest, ground_copy):
        copy.wait_send()
    for result in results:
        result.wait()


def on_device(n_range, n_height, acoustic, mean_wind, ground, shifts):
    _, rows, levels, width = acoustic.shape
    steps = shifts.shape[0]
    hbm = pl.BlockSpec(memory_space=pltpu.HBM)
    return pl.pallas_call(
        functools.partial(kernel, n_range, n_height, steps),
        out_shape=jax.ShapeDtypeStruct(acoustic.shape, jnp.float32),
        in_specs=[pl.BlockSpec(memory_space=pltpu.SMEM), hbm, hbm, hbm],
        out_specs=hbm,
        scratch_shapes=[
            pltpu.VMEM((2, 4, rows + 4, levels, width), jnp.float32),
            pltpu.VMEM(acoustic.shape, jnp.float32),
            pltpu.VMEM(acoustic.shape, jnp.float32),
            pltpu.VMEM((3, rows, levels, width), jnp.float32),
            pltpu.VMEM((3, 2 + SMAX, levels, width), jnp.float32),
            pltpu.VMEM((3, rows + SMAX * steps, levels, width), jnp.float32),
            pltpu.VMEM((rows + SMAX * steps, levels, width), jnp.float32),
            pltpu.VMEM((rows, width), jnp.int32),
            pltpu.VMEM((rows, width), jnp.int32),
            pltpu.VMEM((2, 2, 4, rows, SUB, LANES), jnp.float32),
            pltpu.VMEM((2, 2, 4, rows, SUB, LANES), jnp.float32),
            pltpu.SemaphoreType.DMA((2, 8)),
            pltpu.SemaphoreType.DMA((2, 8)),
            pltpu.SemaphoreType.DMA((3,)),
            pltpu.SemaphoreType.DMA((3,)),
            pltpu.SemaphoreType.DMA((9,)),
        ],
        compiler_params=pltpu.CompilerParams(
            collective_id=0, has_side_effects=True, vmem_limit_bytes=64 * 1024 * 1024 - 65536),
    )(shifts, acoustic, mean_wind, ground)


def solution(mesh):
    spec = P(None, "range", "height", None)
    return jax.shard_map(
        functools.partial(on_device, mesh.shape["range"], mesh.shape["height"]),
        mesh=mesh, in_specs=(spec, spec, P("range", None), P()), out_specs=spec, check_vma=False)
```

```python
import functools

import jax
import jax.numpy as jnp
from jax import lax
from jax.experimental import pallas as pl
from jax.experimental.pallas import tpu as pltpu
from jax.sharding import PartitionSpec as P

SMAX = 2
MESH = pl.DeviceIdType.MESH
LANES = 128
SUB = 8


def kernel(
    n_range, n_height, steps,
    shifts_ref, a_ref, w_in, g_in, o_ref,
    cur, base, acc, own, top, wind, mask, solid, ground, pack, halo, send_sem, recv_sem, wsend, wrecv, local,
):
    rows, levels, width = a_ref.shape[1], a_ref.shape[2], a_ref.shape[3]
    tiles, blocks = levels // SUB, width // LANES
    extra = SMAX * steps
    me, hi = lax.axis_index("range"), lax.axis_index("height")
    below, above = me - 1, me + 1
    wrap_below = lax.rem(me + n_range - 1, n_range)
    wrap_above = lax.rem(me + 1, n_range)
    has_below, has_above = me > 0, me < n_range - 1
    has_down, has_up = hi > 0, hi < n_height - 1

    sub = lax.broadcasted_iota(jnp.int32, (SUB, LANES), 0)
    lane = lax.broadcasted_iota(jnp.int32, (SUB, LANES), 1)

    fetches = [
        pltpu.make_async_copy(a_ref, cur.at[0, :, pl.ds(2, rows)], local.at[0]),
        pltpu.make_async_copy(g_in, solid, local.at[1]),
        pltpu.make_async_copy(a_ref, base, local.at[2]),
        pltpu.make_async_copy(w_in, own, local.at[3]),
        pltpu.make_async_copy(w_in.at[:, pl.ds(rows - 2, 2)], top.at[:, pl.ds(0, 2)], local.at[4]),
        pltpu.make_async_copy(w_in, wind.at[:, pl.ds(0, rows)], local.at[5]),
    ]
    barrier = pltpu.get_barrier_semaphore()
    pl.semaphore_signal(barrier, inc=1, device_id={"range": wrap_below}, device_id_type=MESH)
    pl.semaphore_signal(barrier, inc=1, device_id={"range": wrap_above}, device_id_type=MESH)

    @pl.when(has_down)
    def _():
        pl.semaphore_signal(barrier, inc=1, device_id={"height": hi - 1}, device_id_type=MESH)

    @pl.when(has_up)
    def _():
        pl.semaphore_signal(barrier, inc=1, device_id={"height": hi + 1}, device_id_type=MESH)

    for fetch in fetches:
        fetch.start()

    def pack_row(slot, field, row, low, high):
        down, up = low[0], None
        for j in range(blocks):
            up_j = pltpu.roll(high[j], (2 * j - (SUB - 2)) % SUB, 0)
            if j == 0:
                up = up_j
                continue
            here = (sub >= 2 * j)
            down = jnp.where(here, pltpu.roll(low[j], 2 * j, 0), down)
            up = jnp.where(here, up_j, up)
        pack[slot, 0, field, row] = down
        pack[slot, 1, field, row] = up

    nothing = jnp.zeros((SUB, width), jnp.float32)

    @pl.when(jnp.logical_not(has_below))
    def _():
        for s in range(2):
            for f in range(4):
                for r in range(2):
                    for t in range(tiles):
                        cur[s, f, r, t * SUB:(t + 1) * SUB, :] = nothing

    @pl.when(jnp.logical_not(has_above))
    def _():
        for s in range(2):
            for f in range(4):
                for r in range(2):
                    for t in range(tiles):
                        cur[s, f, rows + 2 + r, t * SUB:(t + 1) * SUB, :] = nothing

    small = jnp.zeros((SUB, LANES), jnp.float32)

    @pl.when(jnp.logical_not(has_down))
    def _():
        for s in range(2):
            for f in range(4):
                for r in range(rows):
                    halo[s, 0, f, r] = small

    @pl.when(jnp.logical_not(has_up))
    def _():
        for s in range(2):
            for f in range(4):
                for r in range(rows):
                    halo[s, 1, f, r] = small

    level = lax.broadcasted_iota(jnp.int32, (SUB, width), 0) + hi * levels

    def flags(row, foot):
        for t in range(tiles):
            mask[row, t * SUB:(t + 1) * SUB, :] = jnp.where(level + t * SUB >= foot, 1.0, 0.0)

    def load_row(row, carry):
        for f in range(4):
            low = [cur[0, f, row + 2, 0:SUB, j * LANES:(j + 1) * LANES] for j in range(blocks)]
            high = [cur[0, f, row + 2, levels - SUB:levels, j * LANES:(j + 1) * LANES] for j in range(blocks)]
            pack_row(0, f, row, low, high)
        return carry

    fetches[0].wait()
    lax.fori_loop(0, rows, load_row, 0)
    fetches[1].wait()
    for r in range(rows):
        flags(r, solid[r:r + 1, :])
    pl.semaphore_wait(barrier, 2 + has_down.astype(jnp.int32) + has_up.astype(jnp.int32))

    def to_below(slot, i):
        return pltpu.make_async_remote_copy(
            src_ref=cur.at[slot, :, pl.ds(2 + i, 1)], dst_ref=cur.at[slot, :, pl.ds(rows + 2 + i, 1)],
            send_sem=send_sem.at[slot, 8 + i], recv_sem=recv_sem.at[slot, 8 + i],
            device_id={"range": below}, device_id_type=MESH)

    def to_above(slot, i):
        return pltpu.make_async_remote_copy(
            src_ref=cur.at[slot, :, pl.ds(rows + i, 1)], dst_ref=cur.at[slot, :, pl.ds(i, 1)],
            send_sem=send_sem.at[slot, i], recv_sem=recv_sem.at[slot, i],
            device_id={"range": above}, device_id_type=MESH)

    spans = [(0, 2), (2, rows - 4), (rows - 2, 2)]

    def to_down(slot, part):
        first, count = spans[part]
        return pltpu.make_async_remote_copy(
            src_ref=pack.at[slot, 0, :, pl.ds(first, count)], dst_ref=halo.at[slot, 1, :, pl.ds(first, count)],
            send_sem=send_sem.at[slot, 2 + part], recv_sem=recv_sem.at[slot, 2 + part],
            device_id={"height": hi - 1}, device_id_type=MESH)

    def to_up(slot, part):
        first, count = spans[part]
        return pltpu.make_async_remote_copy(
            src_ref=pack.at[slot, 1, :, pl.ds(first, count)], dst_ref=halo.at[slot, 0, :, pl.ds(first, count)],
            send_sem=send_sem.at[slot, 5 + part], recv_sem=recv_sem.at[slot, 5 + part],
            device_id={"height": hi + 1}, device_id_type=MESH)

    def send_height(slot, part):
        pl.when(has_down)(lambda: to_down(slot, part).start())
        pl.when(has_up)(lambda: to_up(slot, part).start())

    def recv_height(slot, part):
        pl.when(has_up)(lambda: to_down(slot, part).wait_recv())
        pl.when(has_down)(lambda: to_up(slot, part).wait_recv())

    def drain(slot):
        def down():
            for part in range(3):
                to_down(slot, part).wait_send()

        def up():
            for part in range(3):
                to_up(slot, part).wait_send()

        for i in range(2):
            pl.when(has_below)(lambda i=i: to_below(slot, i).wait_send())
            pl.when(has_above)(lambda i=i: to_above(slot, i).wait_send())
        pl.when(has_down)(down)
        pl.when(has_up)(up)

    wind_first = pltpu.make_async_remote_copy(
        src_ref=w_in.at[:, pl.ds(0, SMAX)], dst_ref=top.at[:, pl.ds(2, SMAX)],
        send_sem=wsend.at[0], recv_sem=wrecv.at[0],
        device_id={"range": wrap_below}, device_id_type=MESH)
    wind_rest = pltpu.make_async_remote_copy(
        src_ref=w_in.at[:, pl.ds(SMAX, extra - SMAX)], dst_ref=wind.at[:, pl.ds(rows + SMAX, extra - SMAX)],
        send_sem=wsend.at[1], recv_sem=wrecv.at[1],
        device_id={"range": wrap_below}, device_id_type=MESH)
    ground_copy = pltpu.make_async_remote_copy(
        src_ref=g_in, dst_ref=ground, send_sem=wsend.at[2], recv_sem=wrecv.at[2],
        device_id={"range": wrap_below}, device_id_type=MESH)

    for i in range(2):
        pl.when(has_below)(lambda i=i: to_below(0, i).start())
        pl.when(has_above)(lambda i=i: to_above(0, i).start())
    for part in (1, 0, 2):
        send_height(0, part)
    ground_copy.start()
    wind_first.start()
    fetches[2].wait()
    fetches[3].wait()

    def stage_row(row, k, step, slot, offset, air, air_row):
        nxt = 1 - slot
        stage = k % 4
        made = {}
        for t in range(tiles):
            level_at = slice(t * SUB, (t + 1) * SUB)
            for j in range(blocks):
                at = slice(j * LANES, (j + 1) * LANES)
                slopes = []
                for f in range(4):
                    c = cur[slot, f, row + 2, level_at, at]
                    d_r = 8.0 * (cur[slot, f, row + 3, level_at, at] - cur[slot, f, row + 1, level_at, at]) - (
                        cur[slot, f, row + 4, level_at, at] - cur[slot, f, row, level_at, at])
                    if j + 1 < blocks:
                        right = cur[slot, f, row + 2, level_at, (j + 1) * LANES:(j + 2) * LANES]
                    else:
                        right = small
                    if j:
                        left = cur[slot, f, row + 2, level_at, (j - 1) * LANES:j * LANES]
                    else:
                        left = small
                    p1 = pltpu.roll(jnp.where(lane < 1, right, c), LANES - 1, 1)
                    p2 = pltpu.roll(jnp.where(lane < 2, right, c), LANES - 2, 1)
                    m1 = pltpu.roll(jnp.where(lane >= LANES - 1, left, c), 1, 1)
                    m2 = pltpu.roll(jnp.where(lane >= LANES - 2, left, c), 2, 1)
                    d_c = 8.0 * (p1 - m1) - (p2 - m2)
                    if t + 1 < tiles:
                        top = cur[slot, f, row + 2, (t + 1) * SUB:(t + 2) * SUB, at]
                    else:
                        top = halo[slot, 1, f, row]
                        if j:
                            top = pltpu.roll(top, SUB - 2 * j, 0)
                    if t:
                        foot = cur[slot, f, row + 2, (t - 1) * SUB:t * SUB, at]
                    else:
                        foot = halo[slot, 0, f, row]
                        if (SUB - 2 - 2 * j) % SUB:
                            foot = pltpu.roll(foot, (SUB - 2 - 2 * j) % SUB, 0)
                    p1 = pltpu.roll(jnp.where(sub < 1, top, c), SUB - 1, 0)
                    p2 = pltpu.roll(jnp.where(sub < 2, top, c), SUB - 2, 0)
                    m1 = pltpu.roll(jnp.where(sub >= SUB - 1, foot, c), 1, 0)
                    m2 = pltpu.roll(jnp.where(sub >= SUB - 2, foot, c), 2, 0)
                    d_h = 8.0 * (p1 - m1) - (p2 - m2)
                    slopes.append((d_r, d_c, d_h))
                a_r = air[0, air_row, level_at, at] - 1.0
                a_c = air[1, air_row, level_at, at]
                a_h = air[2, air_row, level_at, at]
                fluid = mask[row + offset, level_at, at]
                p, u, v, w = slopes
                direct = [u[0] + v[1] + w[2], p[0], p[1], p[2]]
                for f in range(4):
                    d_r, d_c, d_h = slopes[f]
                    change = a_r * d_r + a_c * d_c + a_h * d_h + direct[f]
                    start = base[f, row, level_at, at]
                    if stage == 0:
                        acc[f, row, level_at, at] = change
                    elif stage < 3:
                        acc[f, row, level_at, at] = acc[f, row, level_at, at] + 2.0 * change
                    if stage < 3:
                        new = (start - ((0.4 if stage == 2 else 0.2) / 12.0) * change) * fluid
                    else:
                        new = (start - (0.4 / 72.0) * (acc[f, row, level_at, at] + change)) * fluid
                    if stage == 3 and k < 4 * steps - 1:
                        base[f, row, level_at, at] = new
                    cur[nxt, f, row + 2, level_at, at] = new
                    made[f, t, j] = new
        if k < 4 * steps - 1:
            for f in range(4):
                pack_row(
                    nxt, f, row,
                    [made[f, 0, j] for j in range(blocks)], [made[f, tiles - 1, j] for j in range(blocks)])

    last = 4 * steps - 1
    results = [
        pltpu.make_async_copy(
            cur.at[1 - last % 2, :, pl.ds(2 + first, count)], o_ref.at[:, pl.ds(first, count)], local.at[6 + part])
        for part, (first, count) in enumerate(spans)
    ]
    offset = 0
    for k in range(4 * steps):
        step, slot = k // 4, k % 2
        nxt = 1 - slot
        if k % 4 == 0:
            offset = offset + shifts_ref[step]
        if k == 4:
            fetches[5].wait()
            wind_rest.wait_recv()
            for c in range(3):
                for r in range(SMAX):
                    for t in range(tiles):
                        wind[c, rows + r, t * SUB:(t + 1) * SUB, :] = top[c, 2 + r, t * SUB:(t + 1) * SUB, :]
        if k >= 1:
            drain(nxt)
        offset_now = offset

        def run(part, chosen=None, k=k, step=step, slot=slot, offset_now=offset_now):
            first, count = spans[part]
            if chosen is not None:
                first, count = first + chosen, 1

            def body(i, carry):
                row = first + i
                if step:
                    stage_row(row, k, step, slot, offset_now, wind, row + offset_now)
                elif part < 2:
                    stage_row(row, k, step, slot, offset_now, own, row + offset_now)
                else:
                    stage_row(row, k, step, slot, offset_now, top, row + offset_now - (rows - 2))
                return carry

            lax.fori_loop(0, count, body, 0)

        recv_height(slot, 1)
        run(1)
        if k < last:
            send_height(nxt, 1)
        else:
            results[1].start()
        if k == 1:
            wind_rest.start()
        recv_height(slot, 0)
        for i in range(2):
            pl.when(has_below)(lambda slot=slot, i=i: to_above(slot, i).wait_recv())
        for i in range(2):
            run(0, i)
            if k < last:
                pl.when(has_below)(lambda nxt=nxt, i=i: to_below(nxt, i).start())
        if k < last:
            send_height(nxt, 0)
        else:
            results[0].start()
        recv_height(slot, 2)
        for i in range(2):
            pl.when(has_above)(lambda slot=slot, i=i: to_below(slot, i).wait_recv())
        if k == 0:
            fetches[4].wait()
            wind_first.wait_recv()
            ground_copy.wait_recv()
            for r in range(extra):
                flags(rows + r, ground[r:r + 1, :])
        for i in range(2):
            run(2, i)
            if k < last:
                pl.when(has_above)(lambda nxt=nxt, i=i: to_above(nxt, i).start())
        if k < last:
            send_height(nxt, 2)
        else:
            results[2].start()
    drain(last % 2)
    for copy in (wind_first, wind_rest, ground_copy):
        copy.wait_send()
    for result in results:
        result.wait()


def on_device(n_range, n_height, acoustic, mean_wind, ground, shifts):
    _, rows, levels, width = acoustic.shape
    steps = shifts.shape[0]
    hbm = pl.BlockSpec(memory_space=pltpu.HBM)
    return pl.pallas_call(
        functools.partial(kernel, n_range, n_height, steps),
        out_shape=jax.ShapeDtypeStruct(acoustic.shape, jnp.float32),
        in_specs=[pl.BlockSpec(memory_space=pltpu.SMEM), hbm, hbm, hbm],
        out_specs=hbm,
        scratch_shapes=[
            pltpu.VMEM((2, 4, rows + 4, levels, width), jnp.float32),
            pltpu.VMEM(acoustic.shape, jnp.float32),
            pltpu.VMEM(acoustic.shape, jnp.float32),
            pltpu.VMEM((3, rows, levels, width), jnp.float32),
            pltpu.VMEM((3, 2 + SMAX, levels, width), jnp.float32),
            pltpu.VMEM((3, rows + SMAX * steps, levels, width), jnp.float32),
            pltpu.VMEM((rows + SMAX * steps, levels, width), jnp.float32),
            pltpu.VMEM((rows, width), jnp.int32),
            pltpu.VMEM((rows, width), jnp.int32),
            pltpu.VMEM((2, 2, 4, rows, SUB, LANES), jnp.float32),
            pltpu.VMEM((2, 2, 4, rows, SUB, LANES), jnp.float32),
            pltpu.SemaphoreType.DMA((2, 10)),
            pltpu.SemaphoreType.DMA((2, 10)),
            pltpu.SemaphoreType.DMA((3,)),
            pltpu.SemaphoreType.DMA((3,)),
            pltpu.SemaphoreType.DMA((9,)),
        ],
        compiler_params=pltpu.CompilerParams(
            collective_id=0, has_side_effects=True, vmem_limit_bytes=64 * 1024 * 1024 - 65536),
    )(shifts, acoustic, mean_wind, ground)


def solution(mesh):
    spec = P(None, "range", "height", None)
    return jax.shard_map(
        functools.partial(on_device, mesh.shape["range"], mesh.shape["height"]),
        mesh=mesh, in_specs=(spec, spec, P("range", None), P()), out_specs=spec, check_vma=False)
```
